256 devices in a mesh: dp: 16 (over y_hi, x, core), ctx: 16 (over y_lo, z).
Axes of the slice: x: 4, y: 4 (y_hi: 2, y_lo: 2; y = y_hi * 2 + y_lo), z: 8, core: 2. Of those that a mesh axis runs over, the one named last changes fastest.
Arguments:
- queries: bfloat16 [16, 2048, 36864], P('dp', 'ctx'), may hold values from -70 to 70
- latents: bfloat16 [16, 576, 2048], P('dp', None, 'ctx'), may hold values from -6 to 6
- hidden: bfloat16 [16, 2048, 3584], P('dp', 'ctx'), may hold values from -8 to 8
- key_proj: bfloat16 [3584, 128], replicated, may hold values from -0.09375 to 0.09375
- index_queries: bfloat16 [16, 2048, 8192], P('dp', 'ctx'), may hold values from -0.5 to 0.5
- index_weights: bfloat16 [16, 2048, 64], P('dp', 'ctx'), may hold values from -26 to 26
- doc_start: int32 [16, 32], P('dp'), may hold values from 0 to 31, as said below
Outputs:
- query_loss: float32 [16, 2048], P('dp', 'ctx')
- proj_grad: float32 [3584, 128], P(('dp', 'ctx'))
The draws below stay inside these ranges and needn't reach their ends.
Inputs may be any that keep to these rules, and one draw needn't show every extreme that they name: doc_start[n, 0] = 0 and doc_start[n, 31] = 31; each other entry is either the entry before it or its own block index.
All inputs are finite; a program needn't handle non-finite values.
Results may differ from the reference program's by a relative error of at most 0.008.
The reference program's roundings to bfloat16 on the way count: a program that leaves them out, or rounds other values in their place, can miss the bound.
Values may be sent and summed in bfloat16 or wider, within the bound.
No kernel may reach another device: no remote copies, remote signals or barrier semaphores. Data moves between devices by JAX's collectives and lax.ppermute only.
A program may use at most 256 MiB of HBM per device.

```python
import math
import jax
import jax.numpy as jnp
from jax import lax

H = 64
LAT = 576
IH = 64
ID = 128
DH = 3584
BLK = 64
SEQS = 16
S = 2048
NBLK = 32


def draw_queries(key, part):
    key = jax.random.fold_in(key, 17)
    first_key = jax.random.fold_in(key, 0)
    shape = (SEQS, S, H, LAT)
    values = 0.6 * jax.random.truncated_normal(first_key, -6.0, 6.0, shape, jnp.float32)
    return values.reshape(SEQS, S, H * LAT).astype(jnp.bfloat16)


def draw_index_weights(key, part):
    key = jax.random.fold_in(key, 29)
    first_key = jax.random.fold_in(key, 0)
    shape = (SEQS, S, IH)
    values = 0.25 * jax.random.truncated_normal(first_key, -4.0, 4.0, shape, jnp.float32)
    return values.astype(jnp.bfloat16)


def draw_doc_start(key, part):
    key = jax.random.fold_in(key, 5)
    boundary_marks = jax.random.randint(key, (SEQS, NBLK), 0, 16)
    positions = jnp.arange(NBLK, dtype=jnp.int32)[None, :]
    begins = jnp.where((boundary_marks == 0) | (positions == 0) | (positions == NBLK - 1), positions, 0)
    return lax.cummax(begins, axis=1).astype(jnp.int32)


def strengthened(drawn, rng, source, target, blocks, factor):
    owner, partner = [(jnp.arange(drawn.shape[axis_at]) // (drawn.shape[axis_at] // blocks)).reshape([-1 if axis == axis_at else 1 for axis in range(drawn.ndim)]) for axis_at in (source, target)]
    chosen = jax.random.permutation(rng, blocks)[partner]
    strong = (owner == chosen) | (owner == (partner + blocks // 2) % blocks)
    return jnp.where(strong, factor * drawn, drawn)


def steps_of(key, dims, shards, low, top_value):
    factor_of = 1.0
    for position, shards_of in shards:
        steps = jax.random.uniform(jax.random.fold_in(jax.random.fold_in(key, 6), position), (shards_of,), jnp.float32, low / len(shards), top_value / len(shards))
        factor_of = factor_of * jnp.repeat(jnp.exp(steps), dims[position] // shards_of).reshape((-1,) + (1,) * (len(dims) - 1 - position))
    return factor_of


def normal_values(rng, shape, width, bound, shards=(), kind=jnp.bfloat16):
    loudness = steps_of(rng, shape, shards, -0.22, 0.18) if shards else 1.0
    array = jax.random.normal(rng, shape, jnp.float32) * width * loudness
    return jnp.minimum(jnp.maximum(array, -bound), bound).astype(kind)


def bell_draw_with(rng, extent, scale, limit, cuts, heavy, held_as=jnp.bfloat16):
    drawn = scale * jax.random.normal(rng, extent, jnp.float32)
    if cuts:
        drawn = drawn * steps_of(rng, extent, cuts, -0.22, 0.18)
    return jnp.clip(strengthened(drawn, jax.random.fold_in(rng, 3), *heavy), -limit, limit).astype(held_as)


def setup_inputs(seed: int = 0) -> dict:
    key_of = jax.random.split(jax.random.key(seed), 8)
    return {
        "queries": draw_queries(jax.random.fold_in(key_of[7], 71), 0),
        "latents": normal_values(key_of[1], (SEQS, LAT, S), 1.0, 6.0, ((0, 16), (2, 16))),
        "hidden": bell_draw_with(key_of[2], (SEQS, S, DH), 1.0, 8.0, ((0, 16), (1, 16)), (1, 2, 16, 2.0)),
        "key_proj": normal_values(key_of[3], (DH, ID), DH ** -0.5, 0.09375),
        "index_queries": normal_values(key_of[4], (SEQS, S, IH * ID), 0.0884, 0.5, ((0, 16), (1, 16))),
        "index_weights": draw_index_weights(jax.random.fold_in(key_of[7], 71), 0),
        "doc_start": draw_doc_start(jax.random.fold_in(key_of[7], 71), 0),
    }


SOFT_SCALE = 1.0 / math.sqrt(192.0)

def allowed_pairs(doc_first, total_len):
    row_ids = jnp.arange(total_len, dtype=jnp.int32)
    lower_keys = BLK * jnp.repeat(doc_first, BLK, total_repeat_length=total_len)
    return (row_ids[None, :] <= row_ids[:, None]) & (row_ids[None, :] >= lower_keys[:, None])

def reference(queries, latents, hidden, key_proj, index_queries, index_weights, doc_start):

    def sequence_terms(pieces):
        seq_queries, seq_latents, seq_hidden, seq_index, seq_weights, doc_first = pieces
        total_len = seq_hidden.shape[0]
        block_total = total_len // BLK
        allowed = allowed_pairs(doc_first, total_len)
        latent_floats = seq_latents.astype(jnp.float32)
        per_head = seq_queries.reshape(total_len, H, LAT)

        def add_head(running, head_index):
            single = lax.dynamic_index_in_dim(per_head, head_index, 1, keepdims=False).astype(jnp.float32)
            scores = jnp.dot(single, latent_floats, preferred_element_type=jnp.float32) * SOFT_SCALE
            scores = jnp.where(allowed, scores, -jnp.inf)
            highest = lax.optimization_barrier(jnp.max(scores, axis=1, keepdims=True))
            powers = jnp.exp(scores - highest)
            return (running + powers / lax.optimization_barrier(jnp.sum(powers, axis=1, keepdims=True)), None)
        summed, _ = lax.scan(add_head, jnp.zeros((total_len, total_len), jnp.float32), jnp.arange(H, dtype=jnp.int32))
        target = summed / H
        index_keys = jnp.dot(seq_hidden, key_proj, preferred_element_type=jnp.float32).astype(jnp.bfloat16)
        key_floats = index_keys.astype(jnp.float32)

        def index_block(grad_sum, block_pieces):
            block_queries, block_weights, block_target, block_allowed = block_pieces
            query_floats = block_queries.astype(jnp.float32)
            products = jnp.einsum('qjd,sd->qjs', query_floats, key_floats)
            weights = block_weights.astype(jnp.float32)[:, :, None]
            logits = lax.optimization_barrier(jnp.sum(weights * jnp.maximum(products, 0.0), axis=1))
            logits = jnp.where(block_allowed, logits, -jnp.inf)
            highest = lax.optimization_barrier(jnp.max(logits, axis=1, keepdims=True))
            shifted = logits - highest
            powers = jnp.exp(shifted)
            denominator = lax.optimization_barrier(jnp.sum(powers, axis=1, keepdims=True))
            probabilities = powers / denominator
            log_probs = jnp.where(block_allowed, shifted - jnp.log(denominator), 0.0)
            losses = -lax.optimization_barrier(jnp.sum(block_target * log_probs, axis=1))
            excess = probabilities - block_target
            slopes = jnp.where(products > 0.0, excess[:, None, :] * weights, 0.0).astype(jnp.bfloat16)
            key_terms = jnp.einsum('qjs,qjd->sd', slopes.astype(jnp.float32), query_floats)
            return (grad_sum + key_terms, losses)
        key_grad, losses = lax.scan(index_block, jnp.zeros((total_len, ID), jnp.float32), (seq_index.reshape(block_total, BLK, IH, ID), seq_weights.reshape(block_total, BLK, IH), target.reshape(block_total, BLK, total_len), allowed.reshape(block_total, BLK, total_len)))
        proj_part = jnp.dot(seq_hidden.T, key_grad.astype(jnp.bfloat16), preferred_element_type=jnp.float32)
        return (losses.reshape(total_len), proj_part)
    losses, seq_parts = lax.map(sequence_terms, (queries, latents, hidden, index_queries, index_weights, doc_start))
    return (losses, lax.optimization_barrier(jnp.sum(seq_parts, axis=0)))
```

```python
import functools
import math

import jax
import jax.numpy as jnp
from jax import lax
from jax.experimental import pallas as pl
from jax.experimental.pallas import tpu as pltpu
from jax.sharding import PartitionSpec as P

H = 64
LAT = 576
IH = 64
ID = 128
BLK = 64
ROWS = 128
SOFT_SCALE = 1.0 / math.sqrt(192.0)
EXP2_SCALE = SOFT_SCALE * math.log2(math.e)
LOG2E = math.log2(math.e)
KT = 256
PIECE = LAT + ID
BIG = -1e30
NT = (((1,), (1,)), ((), ()))
SEQ = 2048
SUB = 128
HALF = 8
CHUNK = 32


def not_allowed(table, slot):
    row_start, low_first, low_second = table[0], table[1], table[2]
    keys = table[3 + slot] + lax.broadcasted_iota(jnp.int32, (ROWS, ROWS), 0)
    local = lax.broadcasted_iota(jnp.int32, (ROWS, ROWS), 1)
    low = jnp.where(local < BLK, low_first, low_second)
    return (keys > row_start + local) | (keys < low)


def folded(x, op):
    return op(x.reshape(x.shape[0] // 8, 8, x.shape[1]), axis=0)


def head_pair(queries, pair):
    a = 2 * pair * ID
    return jnp.concatenate([queries[:, a:a + ID], queries[:, a + ID:a + 2 * ID]], 0)


def logits_kernel(*refs):
    pieces, (queries, weights, logits) = refs[:-3], refs[-3:]
    blocks = [piece[base:base + ID, :] for piece in pieces for base in range(LAT, piece.shape[0], PIECE)]
    keys = jnp.concatenate(blocks, 0)
    total = jnp.zeros((keys.shape[0], ROWS), jnp.float32)
    for pair in range(IH // 2):
        inner = lax.dot_general(keys, head_pair(queries, pair), NT, preferred_element_type=jnp.float32)
        inner = jnp.maximum(inner, 0.0)
        total += inner[:, :ROWS] * weights[2 * pair:2 * pair + 1, :]
        total += inner[:, ROWS:] * weights[2 * pair + 1:2 * pair + 2, :]
    logits[...] = total


def target_kernel(table, queries_hbm, *refs):
    accs = [pltpu.ACC(mxu_id=m)((SUB, 2 * ROWS), jnp.float32) for m in range(2) for _ in range(HALF)]
    pl.run_scoped(lambda *acc: target_body((acc[:HALF], acc[HALF:]), table, queries_hbm, *refs), *accs)


def target_body(accs, table, queries_hbm, *refs):
    pieces, logit_parts = refs[:8], refs[8:16]
    losses, excess, queries, lhs, scores, powers, target, sems = refs[16:]
    quad = 4 * LAT
    quads = H // 4

    def quad_copy(q):
        cols = pl.ds(pl.multiple_of(q * quad, 128), quad)
        return pltpu.make_async_copy(queries_hbm.at[:, cols], queries.at[:, cols], sems.at[q])

    for q in range(quads):
        quad_copy(q).start()

    for slot in range(2 * len(pieces)):
        rows = pl.ds(slot * ROWS, ROWS)
        base = (slot % 2) * PIECE
        piece = pieces[slot // 2]
        lat = [piece[base + i * ROWS:base + (i + 1) * ROWS, :] for i in range(4)]
        tail = piece[base + 4 * ROWS:base + LAT, :]
        lat.append(jnp.concatenate([tail[:, :64], tail[:, 64:]], 0))
        blocked = jnp.where(not_allowed(table, slot), 1.0, 0.0).astype(jnp.bfloat16)
        pad = jnp.zeros((ROWS, 64), jnp.bfloat16)
        lhs[0, rows, :] = jnp.concatenate(lat + [pad, blocked], 1)
        lhs[1, rows, :] = jnp.concatenate([pad] + lat + [blocked], 1)
        target[rows, :] = jnp.zeros((ROWS, ROWS), jnp.float32)

    eye = lax.broadcasted_iota(jnp.int32, (ROWS, ROWS), 0) == lax.broadcasted_iota(jnp.int32, (ROWS, ROWS), 1)
    eye = jnp.where(eye, BIG, 0.0).astype(jnp.bfloat16)
    eye = jnp.concatenate([eye, eye], 0)

    def block(g, do_scores, do_powers, do_add, shift, scale):
        sums = [jnp.zeros((8, 4 * ROWS), jnp.float32)]

        def job(t):
            for r in range(0, SUB, CHUNK):
                rows = pl.ds(t * SUB + r, CHUNK)
                if do_add:
                    p = powers[rows, :] * scale
                    p = (p[:, :ROWS] + p[:, ROWS:2 * ROWS]) + (p[:, 2 * ROWS:3 * ROWS] + p[:, 3 * ROWS:])
                    target[rows, :] = target[rows, :] + p
                if do_powers:
                    p = jnp.exp2(scores[rows, :] * EXP2_SCALE - shift)
                    powers[rows, :] = p
                    sums[0] = sums[0] + folded(p, jnp.sum)

        def finish(next_shift):
            next_scale = (1.0 / H) / jnp.sum(sums[0], axis=0, keepdims=True) if do_powers else None
            return next_shift, next_scale

        jobs = [functools.partial(job, t) for t in range(2 * HALF)] if do_powers or do_add else []
        if not do_scores:
            for run in jobs:
                run()
            return finish(None)

        high = [jnp.full((8, 2 * ROWS), -jnp.inf, jnp.float32)] * 2
        step = [0]

        def push(c, staging):
            width = 256 if c < 2 else 128
            for m in range(2):
                start = g * quad + m * 512 + c * 256
                first = pl.ds(pl.multiple_of(start, 128), width)
                second = pl.ds(pl.multiple_of(start + 2 * LAT, 128), width)
                rhs = jnp.concatenate([queries[:, first], queries[:, second]], 0)
                if c == 2:
                    rhs = jnp.concatenate([rhs, eye], 1)
                pltpu.matmul_push_rhs(rhs, staging, m, transpose=True)

        def acc(t, c, load):
            for m in range(2):
                part = lhs[m, t * SUB:(t + 1) * SUB, c * 256:(c + 1) * 256]
                pltpu.matmul_acc_lhs(accs[m][t % HALF], part, load_staged_rhs=load)
            step[0] += 1
            while jobs and len(all_jobs) - len(jobs) < step[0] * len(all_jobs) // (6 * HALF):
                jobs.pop(0)()

        def pop(t):
            for m in range(2):
                v = pltpu.matmul_pop(accs[m][t % HALF])
                scores[t * SUB:(t + 1) * SUB, m * 256:(m + 1) * 256] = v
                high[m] = jnp.maximum(high[m], folded(v, jnp.max))

        all_jobs = list(jobs)
        push(0, 0)
        for t in range(HALF):
            acc(t, 0, 0 if t == 0 else None)
            if t == 0:
                push(1, 1)
        for t in range(HALF):
            acc(t, 1, 1 if t == 0 else None)
            if t == 0:
                push(2, 0)
        for t in range(HALF):
            acc(t, 2, 0 if t == 0 else None)
            if t == 0:
                push(1, 1)
            else:
                pop(t - 1)
        for t in range(HALF, 2 * HALF):
            if t == HALF + 1:
                pop(HALF - 1)
            acc(t, 2, None)
        for t in range(HALF, 2 * HALF):
            acc(t, 1, 1 if t == HALF else None)
            if t == HALF:
                push(0, 0)
        for t in range(HALF, 2 * HALF):
            acc(t, 0, 0 if t == HALF else None)
            if t > HALF:
                pop(t - 1)
        for run in jobs:
            run()
        pop(2 * HALF - 1)
        return finish(jnp.concatenate([jnp.max(h, axis=0, keepdims=True) for h in high], 1) * EXP2_SCALE)

    quad_copy(0).wait()
    shift, _ = block(0, True, False, False, None, None)
    quad_copy(1).wait()
    shift, scale = block(1, True, True, False, shift, None)

    def body(g, carry):
        quad_copy(g).wait()
        return block(g, True, True, True, *carry)

    shift, scale = lax.fori_loop(2, quads, body, (shift, scale))
    _, scale = block(0, False, True, True, shift, scale)
    block(0, False, False, True, None, scale)

    slots = range(2 * len(pieces))
    high = jnp.full((8, ROWS), -jnp.inf, jnp.float32)
    for slot in slots:
        part = logit_parts[slot // 2][(slot % 2) * ROWS:(slot % 2 + 1) * ROWS, :]
        masked = jnp.where(not_allowed(table, slot), BIG, part)
        scores[pl.ds(slot * ROWS, ROWS), :ROWS] = masked
        high = jnp.maximum(high, folded(masked, jnp.max))
    highest = jnp.max(high, axis=0, keepdims=True)

    total = cross = mass = jnp.zeros((8, ROWS), jnp.float32)
    for slot in slots:
        rows = pl.ds(slot * ROWS, ROWS)
        shifted = scores[rows, :ROWS] - highest
        power = jnp.exp2(shifted * LOG2E)
        powers[rows, :ROWS] = power
        total += folded(power, jnp.sum)
        cross += folded(target[rows, :] * shifted, jnp.sum)
        mass += folded(target[rows, :], jnp.sum)
    total = jnp.sum(total, axis=0, keepdims=True)
    cross = jnp.sum(cross, axis=0, keepdims=True)
    mass = jnp.sum(mass, axis=0, keepdims=True)
    losses[...] = mass * jnp.log(total) - cross
    inverse = 1.0 / total
    for slot in slots:
        rows = pl.ds(slot * ROWS, ROWS)
        excess[rows, :] = powers[rows, :ROWS] * inverse - target[rows, :]


def grad_kernel(table, *refs):
    pieces, (excess, queries, weights, key_grad) = refs[:8], refs[8:]
    for index, piece in enumerate(pieces):
        keys = jnp.concatenate([piece[LAT:PIECE, :], piece[PIECE + LAT:, :]], 0)
        part = excess[index * 2 * ROWS:(index + 1) * 2 * ROWS, :]
        grad = jnp.zeros((2 * ROWS, ID), jnp.float32)
        for pair in range(IH // 2):
            pair_queries = head_pair(queries, pair)
            inner = lax.dot_general(keys, pair_queries, NT, preferred_element_type=jnp.float32)
            first = jnp.where(inner[:, :ROWS] > 0.0, part * weights[2 * pair:2 * pair + 1, :], 0.0)
            second = jnp.where(inner[:, ROWS:] > 0.0, part * weights[2 * pair + 1:2 * pair + 2, :], 0.0)
            slopes = jnp.concatenate([first.astype(jnp.bfloat16), second.astype(jnp.bfloat16)], 1)
            grad += jnp.dot(slopes, pair_queries, preferred_element_type=jnp.float32)
        for half in range(2):
            rows = pl.ds(pl.multiple_of(table[3 + 2 * index + half], ROWS), ROWS)
            key_grad[rows, :] = grad[half * ROWS:(half + 1) * ROWS, :].astype(key_grad.dtype)


VM = pl.BlockSpec(memory_space=pltpu.VMEM)
SM = pl.BlockSpec(memory_space=pltpu.SMEM)


def cost(flops, size):
    return pl.CostEstimate(flops=flops, bytes_accessed=size, transcendentals=0)


def index_logits(pieces, index_queries, weights):
    count = sum(piece.shape[0] // PIECE for piece in pieces) * ROWS
    return pl.pallas_call(
        logits_kernel,
        out_shape=jax.ShapeDtypeStruct((count, ROWS), jnp.float32),
        in_specs=[VM] * (len(pieces) + 2),
        out_specs=VM,
        compiler_params=pltpu.CompilerParams(vmem_limit_bytes=32 * 2**20),
        cost_estimate=cost(4 * count * 8192 * 128, 4 * 2**20),
        name="index_logits",
    )(*pieces, index_queries, weights)


def loss_and_excess(table, queries, pieces, logit_parts):
    return pl.pallas_call(
        target_kernel,
        out_shape=(
            jax.ShapeDtypeStruct((1, ROWS), jnp.float32),
            jax.ShapeDtypeStruct((SEQ, ROWS), jnp.float32),
        ),
        in_specs=[SM, pl.BlockSpec(memory_space=pl.ANY)] + [VM] * 16,
        out_specs=(VM, VM),
        scratch_shapes=[
            pltpu.VMEM((ROWS, H * LAT), jnp.bfloat16),
            pltpu.VMEM((2, SEQ, 768), jnp.bfloat16),
            pltpu.VMEM((SEQ, 4 * ROWS), jnp.float32),
            pltpu.VMEM((SEQ, 4 * ROWS), jnp.float32),
            pltpu.VMEM((SEQ, ROWS), jnp.float32),
            pltpu.SemaphoreType.DMA((H // 4,)),
        ],
        compiler_params=pltpu.CompilerParams(vmem_limit_bytes=56 * 2**20),
        cost_estimate=cost(2 * SEQ * 8192 * 768, 16 * 2**20),
        name="loss_and_excess",
    )(table, queries, *pieces, *logit_parts)


def index_grad(table, pieces, excess, index_queries, weights):
    return pl.pallas_call(
        grad_kernel,
        out_shape=jax.ShapeDtypeStruct((SEQ, ID), jnp.bfloat16),
        in_specs=[SM] + [VM] * 11,
        out_specs=VM,
        compiler_params=pltpu.CompilerParams(vmem_limit_bytes=40 * 2**20),
        cost_estimate=cost(4 * SEQ * 8192 * 128, 6 * 2**20),
        name="index_grad",
    )(table, *pieces, excess, index_queries, weights)


def own_piece(latents, own_keys):
    rows = latents.T
    tail = jnp.concatenate([rows[:64, 512:], rows[64:, 512:]], 1)
    return jnp.concatenate([rows[:, i * 128:(i + 1) * 128] for i in range(4)] + [tail, own_keys], 0)


SIDE = 8
ACROSS = [(i, (i + SIDE) % (2 * SIDE)) for i in range(2 * SIDE)]
UP = [(y * SIDE + z, y * SIDE + (z + 1) % SIDE) for y in range(2) for z in range(SIDE)]
DOWN = [(b, a) for a, b in UP]


def shards(queries, latents, hidden, key_proj, index_queries, index_weights, doc_start):
    me = lax.axis_index("ctx")
    side, place = me // SIDE, me % SIDE
    own_hidden = hidden[0]
    own_keys = jnp.dot(own_hidden, key_proj, preferred_element_type=jnp.float32).astype(jnp.bfloat16)
    weights = index_weights[0].T.astype(jnp.float32)
    iq = index_queries[0]

    doc_rows = lax.dynamic_slice_in_dim(doc_start[0], 2 * me, 2, 0) * BLK
    offsets = (place + jnp.arange(SIDE, dtype=jnp.int32)) % SIDE
    starts = (offsets[:, None] + SIDE * jnp.arange(2, dtype=jnp.int32)[None, :]) * ROWS
    table = jnp.concatenate([(me * ROWS)[None], doc_rows, starts.reshape(-1)]).astype(jnp.int32)

    mine = own_piece(latents[0], own_keys)
    other = lax.ppermute(mine, "ctx", ACROSS)
    pair = jnp.where(side == 0, jnp.concatenate([mine, other], 0), jnp.concatenate([other, mine], 0))
    pieces = [pair] + [None] * 7
    logit_parts = [None] * 8
    from_below = from_above = pair
    logit_parts[0] = index_logits([pair], iq, weights)
    for hop in range(1, 4):
        from_below = lax.ppermute(from_below, "ctx", UP)
        from_above = lax.ppermute(from_above, "ctx", DOWN)
        pieces[hop], pieces[8 - hop] = from_above, from_below
        both = index_logits([from_above, from_below], iq, weights)
        logit_parts[hop], logit_parts[8 - hop] = both[:2 * ROWS], both[2 * ROWS:]
    first = lax.ppermute(from_below[:PIECE], "ctx", UP)
    second = lax.ppermute(from_above[PIECE:], "ctx", DOWN)
    pieces[4] = jnp.concatenate([first, second], 0)
    logit_parts[4] = index_logits([first, second], iq, weights)

    losses, excess = loss_and_excess(table, queries[0], pieces, logit_parts)
    key_grad = index_grad(table, pieces, excess, iq, weights)

    key_grad = lax.all_to_all(key_grad, "ctx", 0, 0, tiled=True).reshape(16, ROWS, ID)
    own_grad = jnp.sum(key_grad.astype(jnp.float32), axis=0).astype(jnp.bfloat16)
    proj_part = lax.dot_general(
        own_hidden, own_grad, (((0,), (0,)), ((), ())), preferred_element_type=jnp.float32
    ).astype(jnp.bfloat16)
    proj_part = lax.all_to_all(proj_part, "dp", 0, 0, tiled=True)
    proj_part = jnp.sum(proj_part.reshape(16, -1, ID).astype(jnp.float32), axis=0)
    proj_part = lax.all_to_all(proj_part, "ctx", 0, 0, tiled=True)
    proj_grad = jnp.sum(proj_part.reshape(16, -1, ID), axis=0)
    return (losses, proj_grad)


def solution(mesh):
    return jax.shard_map(
        shards,
        mesh=mesh,
        in_specs=(
            P("dp", "ctx", None),
            P("dp", None, "ctx"),
            P("dp", "ctx", None),
            P(),
            P("dp", "ctx", None),
            P("dp", "ctx", None),
            P("dp", None),
        ),
        out_specs=(P("dp", "ctx"), P(("dp", "ctx"), None)),
        check_vma=False,
    )
```

```python
import functools
import math

import jax
import jax.numpy as jnp
from jax import lax
from jax.experimental import pallas as pl
from jax.experimental.pallas import tpu as pltpu
from jax.sharding import PartitionSpec as P

H = 64
LAT = 576
IH = 64
ID = 128
BLK = 64
ROWS = 128
SOFT_SCALE = 1.0 / math.sqrt(192.0)
EXP2_SCALE = SOFT_SCALE * math.log2(math.e)
LOG2E = math.log2(math.e)
KT = 256
PIECE = LAT + ID
BIG = -1e30
NT = (((1,), (1,)), ((), ()))
PLACES = [(0, 0), (1, 0), (2, 0), (3, 0), (4, 0), (3, 256), (2, 256), (1, 256)]
BITS = [1 << i for i in range(31)] + [-(1 << 31)]
SEQ = 2048
SUB = 128
HALF = 8
SIDE = 8
CHUNK = 32


def block_of(me, slot):
    place = lax.rem(lax.rem(me, SIDE) + slot // 2, SIDE)
    return place + SIDE * (slot % 2)


def not_allowed(me_ref, doc_ref, slot):
    me = me_ref[0]
    keys = block_of(me, slot) * ROWS + lax.broadcasted_iota(jnp.int32, (ROWS, ROWS), 0)
    local = lax.broadcasted_iota(jnp.int32, (ROWS, ROWS), 1)
    low = jnp.where(local < BLK, doc_ref[0, 2 * me] * BLK, doc_ref[0, 2 * me + 1] * BLK)
    return (keys > me * ROWS + local) | (keys < low)


def folded(x, op):
    return op(x.reshape(x.shape[0] // 8, 8, x.shape[1]), axis=0)


def head_pair(queries, pair):
    a = 2 * pair * ID
    return jnp.concatenate([queries[:, a:a + ID], queries[:, a + ID:a + 2 * ID]], 0)


def logits_kernel(*refs):
    pieces, (queries, weights, logits, signs) = refs[:-4], refs[-4:]
    blocks = [piece[base:base + ID, :] for piece in pieces for base in range(LAT, piece.shape[0], PIECE)]
    keys = jnp.concatenate(blocks, 0)
    total = jnp.zeros((keys.shape[0], ROWS), jnp.float32)
    for word in range(2):
        bits = jnp.zeros((keys.shape[0], ROWS), jnp.int32)
        for pair in range(word * IH // 4, (word + 1) * IH // 4):
            inner = lax.dot_general(keys, head_pair(queries, pair), NT, preferred_element_type=jnp.float32)
            for half in range(2):
                head = 2 * pair + half
                part = inner[:, half * ROWS:(half + 1) * ROWS]
                total += jnp.maximum(part, 0.0) * weights[head:head + 1, :]
                bits = bits | jnp.where(part > 0.0, BITS[head % 32], 0)
        signs[word] = bits
    logits[...] = total


def loss_kernel(*refs):
    accs = [pltpu.ACC(mxu_id=m)((SUB, 2 * ROWS), jnp.float32) for m in range(2) for _ in range(HALF)]
    pl.run_scoped(lambda *acc: loss_body((acc[:HALF], acc[HALF:]), *refs), *accs)


def loss_body(accs, me_ref, doc_ref, queries_hbm, *refs):
    pieces, logit_calls, sign_calls, (index_hbm, weights) = refs[:9], refs[9:14], refs[14:19], refs[19:21]
    losses, key_grad, queries, lhs, scores, powers, target, logits, signs, index_queries, sems, more_sems = refs[21:]
    quad = 4 * LAT
    quads = H // 4

    def quad_copy(q):
        cols = pl.ds(pl.multiple_of(q * quad, 128), quad)
        return pltpu.make_async_copy(queries_hbm.at[:, cols], queries.at[:, cols], sems.at[q])

    later = [pltpu.make_async_copy(index_hbm, index_queries, more_sems.at[0])]
    for index, (call, row) in enumerate(PLACES):
        source, rows = pl.ds(row, 2 * ROWS), pl.ds(index * 2 * ROWS, 2 * ROWS)
        later.append(pltpu.make_async_copy(logit_calls[call].at[source, :], logits.at[rows, :], more_sems.at[1 + 2 * index]))
        later.append(
            pltpu.make_async_copy(sign_calls[call].at[:, source, :], signs.at[:, rows, :], more_sems.at[2 + 2 * index])
        )

    for q in range(quads):
        quad_copy(q).start()
    for copy in later:
        copy.start()

    for slot in range(2 * HALF):
        rows = pl.ds(slot * ROWS, ROWS)
        index = slot // 2
        piece = pieces[index if index < 4 else 4 + slot % 2 if index == 4 else index + 1]
        base = 0 if index == 4 else (slot % 2) * PIECE
        lat = [piece[base + i * ROWS:base + (i + 1) * ROWS, :] for i in range(4)]
        tail = piece[base + 4 * ROWS:base + LAT, :]
        lat.append(jnp.concatenate([tail[:, :64], tail[:, 64:]], 0))
        blocked = jnp.where(not_allowed(me_ref, doc_ref, slot), 1.0, 0.0).astype(jnp.bfloat16)
        pad = jnp.zeros((ROWS, 64), jnp.bfloat16)
        lhs[0, rows, :] = jnp.concatenate(lat + [pad, blocked], 1)
        lhs[1, rows, :] = jnp.concatenate([pad] + lat + [blocked], 1)
        target[rows, :] = jnp.zeros((ROWS, ROWS), jnp.float32)

    eye = lax.broadcasted_iota(jnp.int32, (ROWS, ROWS), 0) == lax.broadcasted_iota(jnp.int32, (ROWS, ROWS), 1)
    eye = jnp.where(eye, BIG, 0.0).astype(jnp.bfloat16)
    eye = jnp.concatenate([eye, eye], 0)

    def push(g, c, staging):
        width = 256 if c < 2 else 128
        for m in range(2):
            start = g * quad + m * 512 + c * 256
            first = pl.ds(pl.multiple_of(start, 128), width)
            second = pl.ds(pl.multiple_of(start + 2 * LAT, 128), width)
            rhs = jnp.concatenate([queries[:, first], queries[:, second]], 0)
            if c == 2:
                rhs = jnp.concatenate([rhs, eye], 1)
            pltpu.matmul_push_rhs(rhs, staging, m, transpose=True)

    last = 2 * HALF - 1

    def pop(t, high):
        parts = []
        for m in range(2):
            v = pltpu.matmul_pop(accs[m][t % HALF])
            scores[t * SUB:(t + 1) * SUB, m * 256:(m + 1) * 256] = v
            parts.append(folded(v, jnp.max))
        return jnp.maximum(high, jnp.concatenate(parts, 1))

    def block(g, do_scores, do_powers, do_add, high, scale):
        if do_powers:
            high = pop(last, high)
            shift = jnp.max(high, axis=0, keepdims=True) * EXP2_SCALE
        sums = [jnp.zeros((8, 4 * ROWS), jnp.float32)]

        def job(t):
            for r in range(0, SUB, CHUNK):
                rows = pl.ds(t * SUB + r, CHUNK)
                if do_add:
                    p = powers[rows, :] * scale
                    p = (p[:, :ROWS] + p[:, ROWS:2 * ROWS]) + (p[:, 2 * ROWS:3 * ROWS] + p[:, 3 * ROWS:])
                    target[rows, :] = target[rows, :] + p
                if do_powers:
                    p = jnp.exp2(scores[rows, :] * EXP2_SCALE - shift)
                    powers[rows, :] = p
                    sums[0] = sums[0] + folded(p, jnp.sum)

        jobs = [functools.partial(job, t) for t in range(2 * HALF)] if do_powers or do_add else []
        count = len(jobs)
        done = [0]
        high = jnp.full((8, 4 * ROWS), -jnp.inf, jnp.float32)

        def acc(t, c, load):
            for m in range(2):
                part = lhs[m, t * SUB:(t + 1) * SUB, c * 256:(c + 1) * 256]
                pltpu.matmul_acc_lhs(accs[m][t % HALF], part, load_staged_rhs=load)
            done[0] += 1
            while jobs and count - len(jobs) < done[0] * count // (6 * HALF):
                jobs.pop(0)()

        if do_scores:
            for t in range(HALF):
                acc(t, 0, 0 if t == 0 else None)
                if t == 0:
                    push(g, 1, 1)
            for t in range(HALF):
                acc(t, 1, 1 if t == 0 else None)
                if t == 0:
                    push(g, 2, 0)
            for t in range(HALF):
                acc(t, 2, 0 if t == 0 else None)
                if t == 0:
                    push(g, 1, 1)
                else:
                    high = pop(t - 1, high)
            for t in range(HALF, 2 * HALF):
                if t == HALF + 1:
                    high = pop(HALF - 1, high)
                acc(t, 2, None)
            for t in range(HALF, 2 * HALF):
                acc(t, 1, 1 if t == HALF else None)
                if t == HALF:
                    push(g, 0, 0)
            for t in range(HALF, 2 * HALF):
                acc(t, 0, 0 if t == HALF else None)
                if t == HALF:
                    push(jnp.minimum(g + 1, quads - 1), 0, 0)
                else:
                    high = pop(t - 1, high)
        for run in jobs:
            run()
        scale = (1.0 / H) / jnp.sum(sums[0], axis=0, keepdims=True) if do_powers else None
        return high, scale

    quad_copy(0).wait()
    push(0, 0, 0)
    quad_copy(1).wait()
    high, _ = block(0, True, False, False, None, None)
    quad_copy(2).wait()
    high, scale = block(1, True, True, False, high, None)

    def body(g, carry):
        @pl.when(g < quads - 1)
        def _():
            quad_copy(g + 1).wait()

        return block(g, True, True, True, *carry)

    high, scale = lax.fori_loop(2, quads, body, (high, scale))
    _, scale = block(0, False, True, True, high, scale)
    block(0, False, False, True, None, scale)
    nothing = jnp.zeros((SUB, 256), jnp.bfloat16)
    for m in range(2):
        pltpu.matmul_acc_lhs(accs[m][0], nothing, load_staged_rhs=0)
        pltpu.matmul_pop(accs[m][0])

    for copy in later:
        copy.wait()
    slots = range(2 * HALF)
    high = jnp.full((8, ROWS), -jnp.inf, jnp.float32)
    for slot in slots:
        masked = jnp.where(not_allowed(me_ref, doc_ref, slot), BIG, logits[pl.ds(slot * ROWS, ROWS), :])
        scores[pl.ds(slot * ROWS, ROWS), :ROWS] = masked
        high = jnp.maximum(high, folded(masked, jnp.max))
    highest = jnp.max(high, axis=0, keepdims=True)

    total = cross = mass = jnp.zeros((8, ROWS), jnp.float32)
    for slot in slots:
        rows = pl.ds(slot * ROWS, ROWS)
        shifted = scores[rows, :ROWS] - highest
        power = jnp.exp2(shifted * LOG2E)
        powers[rows, :ROWS] = power
        total += folded(power, jnp.sum)
        cross += folded(target[rows, :] * shifted, jnp.sum)
        mass += folded(target[rows, :], jnp.sum)
    total = jnp.sum(total, axis=0, keepdims=True)
    cross = jnp.sum(cross, axis=0, keepdims=True)
    mass = jnp.sum(mass, axis=0, keepdims=True)
    losses[...] = mass * jnp.log(total) - cross
    inverse = 1.0 / total
    for slot in slots:
        rows = pl.ds(slot * ROWS, ROWS)
        target[rows, :] = powers[rows, :ROWS] * inverse - target[rows, :]

    def pair_step(pair, word):
        cols = pl.ds(pl.multiple_of(2 * pair * ID, 2 * ID), 2 * ID)
        both = index_queries[:, cols]
        rhs = jnp.concatenate([both[:, :ID], both[:, ID:]], 0)
        rhs = jnp.concatenate([rhs, rhs], 1)
        for m in range(2):
            pltpu.matmul_push_rhs(rhs, 0, m)
        pair_weights = [weights[pl.ds(2 * pair + half, 1), :] for half in range(2)]
        flags = [jnp.left_shift(1, lax.rem(2 * pair, 32) + half) for half in range(2)]
        for t in range(HALF):
            for m in range(2):
                slot = m * HALF + t
                bits = signs[word, pl.ds(slot * ROWS, ROWS), :]
                part = target[pl.ds(slot * ROWS, ROWS), :]
                slopes = [
                    jnp.where((bits & flags[half]) != 0, part * pair_weights[half], 0.0).astype(jnp.bfloat16)
                    for half in range(2)
                ]
                pltpu.matmul_acc_lhs(accs[m][t], jnp.concatenate(slopes, 1), load_staged_rhs=0 if t == 0 else None)

    for word in range(2):
        def step(pair, _, word=word):
            pair_step(pair, word)
            return 0

        lax.fori_loop(word * IH // 4, (word + 1) * IH // 4, step, 0)

    for slot in range(2 * HALF):
        rows = pl.ds(pl.multiple_of(block_of(me_ref[0], slot) * ROWS, ROWS), ROWS)
        grad = pltpu.matmul_pop(accs[slot // HALF][slot % HALF])
        key_grad[rows, :] = grad[:, :ID].astype(key_grad.dtype)


def piece_kernel(hidden, key_proj, latents, piece):
    keys = jnp.dot(hidden[...], key_proj[...], preferred_element_type=jnp.float32)
    piece[LAT:, :] = keys.astype(jnp.bfloat16)
    for i in range(4):
        piece[i * ROWS:(i + 1) * ROWS, :] = latents[i * ROWS:(i + 1) * ROWS, :].T
    tail = latents[4 * ROWS:, :].T
    piece[4 * ROWS:LAT, :] = jnp.concatenate([tail[:64, :], tail[64:, :]], 1)


def pair_kernel(me_ref, mine, other, pair):
    first = me_ref[0] < SIDE

    @pl.when(first)
    def _():
        pair[:PIECE, :] = mine[...]
        pair[PIECE:, :] = other[...]

    @pl.when(jnp.logical_not(first))
    def _():
        pair[:PIECE, :] = other[...]
        pair[PIECE:, :] = mine[...]


VM = pl.BlockSpec(memory_space=pltpu.VMEM)
SM = pl.BlockSpec(memory_space=pltpu.SMEM)


def cost(flops, size):
    return pl.CostEstimate(flops=flops, bytes_accessed=size, transcendentals=0)


def own_piece(hidden, key_proj, latents):
    return pl.pallas_call(
        piece_kernel,
        out_shape=jax.ShapeDtypeStruct((PIECE, ROWS), jnp.bfloat16),
        in_specs=[VM] * 3,
        out_specs=VM,
        compiler_params=pltpu.CompilerParams(vmem_limit_bytes=16 * 2**20),
        name="own_piece",
    )(hidden, key_proj, latents)


def both_pieces(me, mine, other):
    return pl.pallas_call(
        pair_kernel,
        out_shape=jax.ShapeDtypeStruct((2 * PIECE, ROWS), jnp.bfloat16),
        in_specs=[SM, VM, VM],
        out_specs=VM,
        name="both_pieces",
    )(me, mine, other)


def index_logits(pieces, index_queries, weights):
    count = sum(piece.shape[0] // PIECE for piece in pieces) * ROWS
    return pl.pallas_call(
        logits_kernel,
        out_shape=(
            jax.ShapeDtypeStruct((count, ROWS), jnp.float32),
            jax.ShapeDtypeStruct((2, count, ROWS), jnp.int32),
        ),
        in_specs=[VM] * (len(pieces) + 2),
        out_specs=(VM, VM),
        compiler_params=pltpu.CompilerParams(vmem_limit_bytes=32 * 2**20),
        cost_estimate=cost(4 * count * 8192 * 128, 4 * 2**20),
        name="index_logits",
    )(*pieces, index_queries, weights)


def loss_and_grad(me, docs, queries, pieces, calls, index_queries, weights):
    anywhere = pl.BlockSpec(memory_space=pl.ANY)
    return pl.pallas_call(
        loss_kernel,
        out_shape=(
            jax.ShapeDtypeStruct((1, ROWS), jnp.float32),
            jax.ShapeDtypeStruct((SEQ, ID), jnp.bfloat16),
        ),
        in_specs=[SM, SM, anywhere] + [VM] * 9 + [anywhere] * 11 + [VM],
        out_specs=(VM, VM),
        scratch_shapes=[
            pltpu.VMEM((ROWS, H * LAT), jnp.bfloat16),
            pltpu.VMEM((2, SEQ, 768), jnp.bfloat16),
            pltpu.VMEM((SEQ, 4 * ROWS), jnp.float32),
            pltpu.VMEM((SEQ, 4 * ROWS), jnp.float32),
            pltpu.VMEM((SEQ, ROWS), jnp.float32),
            pltpu.VMEM((SEQ, ROWS), jnp.float32),
            pltpu.VMEM((2, SEQ, ROWS), jnp.int32),
            pltpu.VMEM((ROWS, IH * ID), jnp.bfloat16),
            pltpu.SemaphoreType.DMA((H // 4,)),
            pltpu.SemaphoreType.DMA((17,)),
        ],
        compiler_params=pltpu.CompilerParams(vmem_limit_bytes=52 * 2**20),
        cost_estimate=cost(2 * SEQ * 8192 * 1024, 16 * 2**20),
        name="loss_and_grad",
    )(me, docs, queries, *pieces, *[call[0] for call in calls], *[call[1] for call in calls], index_queries, weights)


ACROSS = [(i, (i + SIDE) % (2 * SIDE)) for i in range(2 * SIDE)]
UP = [(y * SIDE + z, y * SIDE + (z + 1) % SIDE) for y in range(2) for z in range(SIDE)]
DOWN = [(b, a) for a, b in UP]


PARTNER = [(i, (i + 8) % 16) for i in range(16)]
GROUPS = [list(range(8)), list(range(8, 16))]


def shards(queries, latents, hidden, key_proj, index_queries, index_weights, doc_start):
    me = lax.axis_index("ctx").astype(jnp.int32).reshape(1)
    own_hidden = hidden[0]
    features = own_hidden.shape[1] // 2
    weights = index_weights[0].T.astype(jnp.float32)
    iq = index_queries[0]

    mine = own_piece(own_hidden, key_proj, latents[0])
    other = lax.ppermute(mine, "ctx", ACROSS)
    pair = both_pieces(me, mine, other)
    upper = lax.axis_index("dp") >= 8
    kept = jnp.where(upper, own_hidden[:, features:], own_hidden[:, :features])
    given = jnp.where(upper, own_hidden[:, :features], own_hidden[:, features:])
    taken = lax.ppermute(given, "dp", PARTNER)
    above, below = [pair], [pair]
    calls = []
    for hop in range(1, 5):
        if hop < 4:
            next_below = lax.ppermute(below[-1], "ctx", UP)
            next_above = lax.ppermute(above[-1], "ctx", DOWN)
        else:
            next_below = lax.ppermute(below[-1][:PIECE], "ctx", UP)
            next_above = lax.ppermute(above[-1][PIECE:], "ctx", DOWN)
        call = index_logits([pair] if hop == 1 else [above[-1], below[-1]], iq, weights)
        next_below, next_above, call = lax.optimization_barrier((next_below, next_above, call))
        below.append(next_below)
        above.append(next_above)
        calls.append(call)
    calls.append(index_logits([below[4], above[4]], iq, weights))
    pieces = above[:4] + [below[4], above[4]] + below[3:0:-1]
    losses, key_grad = loss_and_grad(me, doc_start, queries[0], pieces, calls, iq, weights)

    key_grad = lax.all_to_all(key_grad, "ctx", 0, 0, tiled=True).reshape(16, ROWS, ID)
    own_grad = jnp.sum(key_grad.astype(jnp.float32), axis=0).astype(jnp.bfloat16)
    other_grad = lax.ppermute(own_grad, "dp", PARTNER)
    proj_part = lax.dot_general(
        jnp.concatenate([kept, taken], 0), jnp.concatenate([own_grad, other_grad], 0),
        (((0,), (0,)), ((), ())), preferred_element_type=jnp.float32,
    ).astype(jnp.bfloat16)
    proj_part = lax.all_to_all(proj_part, "dp", 0, 0, tiled=True, axis_index_groups=GROUPS)
    proj_part = jnp.sum(proj_part.reshape(8, -1, ID).astype(jnp.float32), axis=0)
    proj_part = lax.all_to_all(proj_part, "ctx", 0, 0, tiled=True)
    proj_grad = jnp.sum(proj_part.reshape(16, -1, ID), axis=0)
    return (losses, proj_grad)


def solution(mesh):
    return jax.shard_map(
        shards,
        mesh=mesh,
        in_specs=(
            P("dp", "ctx", None),
            P("dp", None, "ctx"),
            P("dp", "ctx", None),
            P(),
            P("dp", "ctx", None),
            P("dp", "ctx", None),
            P("dp", None),
        ),
        out_specs=(P("dp", "ctx"), P(("dp", "ctx"), None)),
        check_vma=False,
    )
```

```python
import functools
import math

import jax
import jax.numpy as jnp
from jax import lax
from jax.experimental import pallas as pl
from jax.experimental.pallas import tpu as pltpu
from jax.sharding import PartitionSpec as P

H = 64
LAT = 576
IH = 64
ID = 128
BLK = 64
ROWS = 128
SOFT_SCALE = 1.0 / math.sqrt(192.0)
EXP2_SCALE = SOFT_SCALE * math.log2(math.e)
LOG2E = math.log2(math.e)
KT = 256
PIECE = LAT + ID
BIG = -1e30
NT = (((1,), (1,)), ((), ()))
PLACES = [(0, 0), (1, 0), (2, 0), (3, 0), (4, 0), (3, 256), (2, 256), (1, 256)]
BITS = [1 << i for i in range(31)] + [-(1 << 31)]
SEQ = 2048
SUB = 128
HALF = 8
SIDE = 8
CHUNK = 32


def block_of(me, slot):
    place = lax.rem(lax.rem(me, SIDE) + slot // 2, SIDE)
    side = lax.div(me, SIDE)
    return place + SIDE * (side if slot % 2 == 0 else 1 - side)


def not_allowed(me_ref, doc_ref, slot):
    me = me_ref[0]
    keys = block_of(me, slot) * ROWS + lax.broadcasted_iota(jnp.int32, (ROWS, ROWS), 0)
    local = lax.broadcasted_iota(jnp.int32, (ROWS, ROWS), 1)
    low = jnp.where(local < BLK, doc_ref[0, 2 * me] * BLK, doc_ref[0, 2 * me + 1] * BLK)
    return (keys > me * ROWS + local) | (keys < low)


def folded(x, op):
    return op(x.reshape(x.shape[0] // 8, 8, x.shape[1]), axis=0)


def head_pair(queries, pair):
    a = 2 * pair * ID
    return jnp.concatenate([queries[:, a:a + ID], queries[:, a + ID:a + 2 * ID]], 0)


def logits_kernel(*refs):
    pieces, (queries, weights, logits_hbm, signs_hbm, logits, signs, sems) = refs[:-7], refs[-7:]
    copies = []
    keys = jnp.concatenate([piece[LAT:, :] for piece in pieces], 0)
    total = jnp.zeros((keys.shape[0], ROWS), jnp.float32)
    for word in range(2):
        bits = jnp.zeros((keys.shape[0], ROWS), jnp.int32)
        for pair in range(word * IH // 4, (word + 1) * IH // 4):
            inner = lax.dot_general(keys, head_pair(queries, pair), NT, preferred_element_type=jnp.float32)
            for half in range(2):
                head = 2 * pair + half
                part = inner[:, half * ROWS:(half + 1) * ROWS]
                total += jnp.maximum(part, 0.0) * weights[head:head + 1, :]
                bits = bits | jnp.where(part > 0.0, BITS[head % 32], 0)
        signs[word] = bits
        copies.append(pltpu.make_async_copy(signs.at[word], signs_hbm.at[word], sems.at[word]))
        copies[-1].start()
    logits[...] = total
    copies.append(pltpu.make_async_copy(logits, logits_hbm, sems.at[2]))
    copies[-1].start()
    for copy in copies:
        copy.wait()


def loss_kernel(*refs):
    accs = [pltpu.ACC(mxu_id=m)((SUB, 2 * ROWS), jnp.float32) for m in range(2) for _ in range(HALF)]
    pl.run_scoped(lambda *acc: loss_body((acc[:HALF], acc[HALF:]), *refs), *accs)


def loss_body(accs, me_ref, doc_ref, queries_hbm, *refs):
    pieces, logit_calls, sign_calls, (index_hbm, weights) = refs[:16], refs[16:21], refs[21:26], refs[26:28]
    losses, key_grad, queries, lhs, scores, powers, target, logits, probs, signs, index_queries, parts, sems, more_sems, part_sems = refs[28:]
    quad = 4 * LAT
    quads = H // 4

    def quad_copy(q):
        cols = pl.ds(pl.multiple_of(q * quad, 128), quad)
        return pltpu.make_async_copy(queries_hbm.at[:, cols], queries.at[:, cols], sems.at[q])

    early = []
    later = [pltpu.make_async_copy(index_hbm, index_queries, more_sems.at[0])]
    for index, (call, row) in enumerate(PLACES):
        source, rows = pl.ds(row, 2 * ROWS), pl.ds(index * 2 * ROWS, 2 * ROWS)
        early.append(pltpu.make_async_copy(logit_calls[call].at[source, :], logits.at[rows, :], more_sems.at[1 + 2 * index]))
        later.append(
            pltpu.make_async_copy(sign_calls[call].at[:, source, :], signs.at[:, rows, :], more_sems.at[2 + 2 * index])
        )

    part_copies = [pltpu.make_async_copy(piece, parts.at[i], part_sems.at[i]) for i, piece in enumerate(pieces)]
    for copy in part_copies:
        copy.start()
    for q in range(2):
        quad_copy(q).start()
    for copy in early:
        copy.start()

    for slot in range(2 * HALF):
        rows = pl.ds(slot * ROWS, ROWS)
        part_copies[slot].wait()
        lat = [parts[slot, i * ROWS:(i + 1) * ROWS, :] for i in range(4)]
        tail = parts[slot, 4 * ROWS:LAT, :]
        lat.append(jnp.concatenate([tail[:, :64], tail[:, 64:]], 0))
        blocked = jnp.where(not_allowed(me_ref, doc_ref, slot), 1.0, 0.0).astype(jnp.bfloat16)
        pad = jnp.zeros((ROWS, 64), jnp.bfloat16)
        lhs[0, rows, :] = jnp.concatenate(lat + [pad, blocked], 1)
        lhs[1, rows, :] = jnp.concatenate([pad] + lat + [blocked], 1)
        target[rows, :] = jnp.zeros((ROWS, ROWS), jnp.float32)

    eye = lax.broadcasted_iota(jnp.int32, (ROWS, ROWS), 0) == lax.broadcasted_iota(jnp.int32, (ROWS, ROWS), 1)
    eye = jnp.where(eye, BIG, 0.0).astype(jnp.bfloat16)
    eye = jnp.concatenate([eye, eye], 0)

    def push(g, c, staging):
        width = 256 if c < 2 else 128
        for m in range(2):
            start = g * quad + m * 512 + c * 256
            first = pl.ds(pl.multiple_of(start, 128), width)
            second = pl.ds(pl.multiple_of(start + 2 * LAT, 128), width)
            rhs = jnp.concatenate([queries[:, first], queries[:, second]], 0)
            if c == 2:
                rhs = jnp.concatenate([rhs, eye], 1)
            pltpu.matmul_push_rhs(rhs, staging, m, transpose=True)

    last = 2 * HALF - 1

    def pop(t, high):
        parts = []
        for m in range(2):
            v = pltpu.matmul_pop(accs[m][t % HALF])
            scores[t * SUB:(t + 1) * SUB, m * 256:(m + 1) * 256] = v
            parts.append(folded(v, jnp.max))
        return jnp.maximum(high, jnp.concatenate(parts, 1))

    def block(g, do_scores, do_powers, do_add, high, scale, extra=()):
        if do_powers:
            high = pop(last, high)
            shift = jnp.max(high, axis=0, keepdims=True) * EXP2_SCALE
        sums = [jnp.zeros((8, 4 * ROWS), jnp.float32)]

        def job(t):
            for r in range(0, SUB, CHUNK):
                rows = pl.ds(t * SUB + r, CHUNK)
                if do_add:
                    p = powers[rows, :] * scale
                    p = (p[:, :ROWS] + p[:, ROWS:2 * ROWS]) + (p[:, 2 * ROWS:3 * ROWS] + p[:, 3 * ROWS:])
                    target[rows, :] = target[rows, :] + p
                if do_powers:
                    p = jnp.exp2(scores[rows, :] * EXP2_SCALE - shift)
                    powers[rows, :] = p
                    sums[0] = sums[0] + folded(p, jnp.sum)

        jobs = [functools.partial(job, t) for t in range(2 * HALF)] if do_powers or do_add else []
        jobs = jobs + list(extra)
        count = len(jobs)
        done = [0]
        high = jnp.full((8, 4 * ROWS), -jnp.inf, jnp.float32)

        def acc(t, c, load):
            for m in range(2):
                part = lhs[m, t * SUB:(t + 1) * SUB, c * 256:(c + 1) * 256]
                pltpu.matmul_acc_lhs(accs[m][t % HALF], part, load_staged_rhs=load)
            done[0] += 1
            while jobs and count - len(jobs) < done[0] * count // (6 * HALF):
                jobs.pop(0)()

        if do_scores:
            for t in range(HALF):
                acc(t, 0, 0 if t == 0 else None)
                if t == 0:
                    push(g, 1, 1)
            for t in range(HALF):
                acc(t, 1, 1 if t == 0 else None)
                if t == 0:
                    push(g, 2, 0)
            for t in range(HALF):
                acc(t, 2, 0 if t == 0 else None)
                if t == 0:
                    push(g, 1, 1)
                else:
                    high = pop(t - 1, high)
            for t in range(HALF, 2 * HALF):
                if t == HALF + 1:
                    high = pop(HALF - 1, high)
                acc(t, 2, None)
            for t in range(HALF, 2 * HALF):
                acc(t, 1, 1 if t == HALF else None)
                if t == HALF:
                    push(g, 0, 0)
            for t in range(HALF, 2 * HALF):
                acc(t, 0, 0 if t == HALF else None)
                if t == HALF:
                    push(jnp.minimum(g + 1, quads - 1), 0, 0)
                else:
                    high = pop(t - 1, high)
        for run in jobs:
            run()
        scale = (1.0 / H) / jnp.sum(sums[0], axis=0, keepdims=True) if do_powers else None
        return high, scale

    logit_high = [jnp.full((8, ROWS), -jnp.inf, jnp.float32)]
    logit_sum = [jnp.zeros((8, ROWS), jnp.float32)]

    def mask_job(slot):
        rows = pl.ds(slot * ROWS, ROWS)
        masked = jnp.where(not_allowed(me_ref, doc_ref, slot), BIG, logits[rows, :])
        logits[rows, :] = masked
        logit_high[0] = jnp.maximum(logit_high[0], folded(masked, jnp.max))

    def prob_job(slot):
        rows = pl.ds(slot * ROWS, ROWS)
        power = jnp.exp2((logits[rows, :] - highest) * LOG2E)
        probs[rows, :] = power
        logit_sum[0] = logit_sum[0] + folded(power, jnp.sum)

    quad_copy(0).wait()
    push(0, 0, 0)
    for q in range(2, 4):
        quad_copy(q).start()
    for copy in early:
        copy.wait()
    quad_copy(1).wait()
    high, _ = block(0, True, False, False, None, None, [functools.partial(mask_job, t) for t in range(2 * HALF)])
    highest = jnp.max(logit_high[0], axis=0, keepdims=True)
    for copy in later:
        copy.start()
    quad_copy(4).start()
    quad_copy(2).wait()
    high, scale = block(1, True, True, False, high, None, [functools.partial(prob_job, t) for t in range(2 * HALF)])

    def body(g, carry):
        @pl.when(g < quads - 3)
        def _():
            quad_copy(g + 3).start()

        @pl.when(g < quads - 1)
        def _():
            quad_copy(g + 1).wait()

        return block(g, True, True, True, *carry)

    high, scale = lax.fori_loop(2, quads, body, (high, scale))
    _, scale = block(0, False, True, True, high, scale)
    block(0, False, False, True, None, scale)
    nothing = jnp.zeros((SUB, 256), jnp.bfloat16)
    for m in range(2):
        pltpu.matmul_acc_lhs(accs[m][0], nothing, load_staged_rhs=0)
        pltpu.matmul_pop(accs[m][0])

    total = jnp.sum(logit_sum[0], axis=0, keepdims=True)
    inverse = 1.0 / total
    cross = mass = jnp.zeros((8, ROWS), jnp.float32)
    for slot in range(2 * HALF):
        rows = pl.ds(slot * ROWS, ROWS)
        aim = target[rows, :]
        cross += folded(aim * (logits[rows, :] - highest), jnp.sum)
        mass += folded(aim, jnp.sum)
        target[rows, :] = probs[rows, :] * inverse - aim
    cross = jnp.sum(cross, axis=0, keepdims=True)
    mass = jnp.sum(mass, axis=0, keepdims=True)
    losses[...] = mass * jnp.log(total) - cross
    for copy in later:
        copy.wait()

    def pair_step(pair, word):
        cols = pl.ds(pl.multiple_of(2 * pair * ID, 2 * ID), 2 * ID)
        both = index_queries[:, cols]
        rhs = jnp.concatenate([both[:, :ID], both[:, ID:]], 0)
        rhs = jnp.concatenate([rhs, rhs], 1)
        for m in range(2):
            pltpu.matmul_push_rhs(rhs, 0, m)
        pair_weights = [weights[pl.ds(2 * pair + half, 1), :] for half in range(2)]
        flags = [jnp.left_shift(1, lax.rem(2 * pair, 32) + half) for half in range(2)]
        for t in range(HALF):
            for m in range(2):
                slot = m * HALF + t
                bits = signs[word, pl.ds(slot * ROWS, ROWS), :]
                part = target[pl.ds(slot * ROWS, ROWS), :]
                slopes = [
                    jnp.where((bits & flags[half]) != 0, part * pair_weights[half], 0.0).astype(jnp.bfloat16)
                    for half in range(2)
                ]
                pltpu.matmul_acc_lhs(accs[m][t], jnp.concatenate(slopes, 1), load_staged_rhs=0 if t == 0 else None)

    for word in range(2):
        def step(pair, _, word=word):
            pair_step(pair, word)
            return 0

        lax.fori_loop(word * IH // 4, (word + 1) * IH // 4, step, 0)

    for slot in range(2 * HALF):
        rows = pl.ds(pl.multiple_of(block_of(me_ref[0], slot) * ROWS, ROWS), ROWS)
        grad = pltpu.matmul_pop(accs[slot // HALF][slot % HALF])
        key_grad[rows, :] = grad[:, :ID].astype(key_grad.dtype)


def piece_kernel(hidden, key_proj, latents, piece):
    keys = jnp.dot(hidden[...], key_proj[...], preferred_element_type=jnp.float32)
    piece[LAT:, :] = keys.astype(jnp.bfloat16)
    for i in range(4):
        piece[i * ROWS:(i + 1) * ROWS, :] = latents[i * ROWS:(i + 1) * ROWS, :].T
    tail = latents[4 * ROWS:, :].T
    piece[4 * ROWS:LAT, :] = jnp.concatenate([tail[:64, :], tail[64:, :]], 1)


def split_kernel(core_ref, hidden, kept, given):
    width = hidden.shape[1] // 16
    parts = [hidden[:, i * width:(i + 1) * width] for i in range(16)]
    even, odd = jnp.concatenate(parts[::2], 1), jnp.concatenate(parts[1::2], 1)

    @pl.when(core_ref[0] == 0)
    def _():
        kept[...] = even
        given[...] = odd

    @pl.when(core_ref[0] != 0)
    def _():
        kept[...] = odd
        given[...] = even


VM = pl.BlockSpec(memory_space=pltpu.VMEM)
SM = pl.BlockSpec(memory_space=pltpu.SMEM)


def cost(flops, size):
    return pl.CostEstimate(flops=flops, bytes_accessed=size, transcendentals=0)


def own_piece(hidden, key_proj, latents):
    return pl.pallas_call(
        piece_kernel,
        out_shape=jax.ShapeDtypeStruct((PIECE, ROWS), jnp.bfloat16),
        in_specs=[VM] * 3,
        out_specs=VM,
        compiler_params=pltpu.CompilerParams(vmem_limit_bytes=16 * 2**20),
        name="own_piece",
    )(hidden, key_proj, latents)


def split_features(core, hidden):
    half = jax.ShapeDtypeStruct((hidden.shape[0], hidden.shape[1] // 2), jnp.bfloat16)
    return pl.pallas_call(
        split_kernel,
        out_shape=(half, half),
        in_specs=[SM, VM],
        out_specs=(VM, VM),
        compiler_params=pltpu.CompilerParams(vmem_limit_bytes=16 * 2**20),
        cost_estimate=cost(0, 2 * 2**20),
        name="split_features",
    )(core, hidden)


def index_logits(pieces, index_queries, weights):
    count = len(pieces) * ROWS
    return pl.pallas_call(
        logits_kernel,
        out_shape=(
            jax.ShapeDtypeStruct((count, ROWS), jnp.float32),
            jax.ShapeDtypeStruct((2, count, ROWS), jnp.int32),
        ),
        in_specs=[VM] * (len(pieces) + 2),
        out_specs=(pl.BlockSpec(memory_space=pltpu.HBM),) * 2,
        scratch_shapes=[
            pltpu.VMEM((count, ROWS), jnp.float32),
            pltpu.VMEM((2, count, ROWS), jnp.int32),
            pltpu.SemaphoreType.DMA((3,)),
        ],
        compiler_params=pltpu.CompilerParams(vmem_limit_bytes=32 * 2**20),
        cost_estimate=cost(4 * count * 8192 * 128, 4 * 2**20),
        name="index_logits",
    )(*pieces, index_queries, weights)


def loss_and_grad(me, docs, queries, pieces, calls, index_queries, weights):
    anywhere = pl.BlockSpec(memory_space=pl.ANY)
    return pl.pallas_call(
        loss_kernel,
        out_shape=(
            jax.ShapeDtypeStruct((1, ROWS), jnp.float32),
            jax.ShapeDtypeStruct((SEQ, ID), jnp.bfloat16),
        ),
        in_specs=[SM, SM, anywhere] + [anywhere] * 27 + [VM],
        out_specs=(VM, VM),
        scratch_shapes=[
            pltpu.VMEM((ROWS, H * LAT), jnp.bfloat16),
            pltpu.VMEM((2, SEQ, 768), jnp.bfloat16),
            pltpu.VMEM((SEQ, 4 * ROWS), jnp.float32),
            pltpu.VMEM((SEQ, 4 * ROWS), jnp.float32),
            pltpu.VMEM((SEQ, ROWS), jnp.float32),
            pltpu.VMEM((SEQ, ROWS), jnp.float32),
            pltpu.VMEM((SEQ, ROWS), jnp.float32),
            pltpu.VMEM((2, SEQ, ROWS), jnp.int32),
            pltpu.VMEM((ROWS, IH * ID), jnp.bfloat16),
            pltpu.VMEM((2 * HALF, PIECE, ROWS), jnp.bfloat16),
            pltpu.SemaphoreType.DMA((H // 4,)),
            pltpu.SemaphoreType.DMA((17,)),
            pltpu.SemaphoreType.DMA((2 * HALF,)),
        ],
        compiler_params=pltpu.CompilerParams(vmem_limit_bytes=62 * 2**20),
        cost_estimate=cost(2 * SEQ * 8192 * 1024, 16 * 2**20),
        name="loss_and_grad",
    )(me, docs, queries, *pieces, *[call[0] for call in calls], *[call[1] for call in calls], index_queries, weights)


ACROSS = [(i, (i + SIDE) % (2 * SIDE)) for i in range(2 * SIDE)]
UP = [(y * SIDE + z, y * SIDE + (z + 1) % SIDE) for y in range(2) for z in range(SIDE)]
DOWN = [(b, a) for a, b in UP]


CORES = [(i, i ^ 1) for i in range(16)]
GROUPS = [list(range(0, 16, 2)), list(range(1, 16, 2))]


def shards(queries, latents, hidden, key_proj, index_queries, index_weights, doc_start):
    me = lax.axis_index("ctx").astype(jnp.int32).reshape(1)
    core = lax.rem(lax.axis_index("dp"), 2).astype(jnp.int32).reshape(1)
    own_hidden = hidden[0]
    weights = index_weights[0].T.astype(jnp.float32)
    iq = index_queries[0]

    blocks = [[None, None] for _ in range(SIDE)]
    mine = own_piece(own_hidden, key_proj, latents[0])
    blocks[0][0] = mine
    blocks[7][0] = lax.ppermute(mine, "ctx", UP)
    blocks[1][0] = lax.ppermute(mine, "ctx", DOWN)
    blocks[0][1] = lax.ppermute(mine, "ctx", ACROSS)
    kept, given = split_features(core, own_hidden)
    taken = lax.ppermute(given, "dp", CORES)
    calls = []
    for hop in range(1, 5):
        if hop == 4:
            blocks[4][0] = lax.ppermute(blocks[5][0], "ctx", UP)
            blocks[4][1] = lax.ppermute(blocks[3][1], "ctx", DOWN)
        else:
            if hop > 1:
                blocks[8 - hop][0] = lax.ppermute(blocks[9 - hop][0], "ctx", UP)
                blocks[hop][0] = lax.ppermute(blocks[hop - 1][0], "ctx", DOWN)
            blocks[8 - hop][1] = lax.ppermute(blocks[(9 - hop) % 8][1], "ctx", UP)
            blocks[hop][1] = lax.ppermute(blocks[hop - 1][1], "ctx", DOWN)
        call = index_logits(blocks[0] if hop == 1 else blocks[hop - 1] + blocks[9 - hop], iq, weights)
        blocks[hop][1], blocks[8 - hop][1], call = lax.optimization_barrier((blocks[hop][1], blocks[8 - hop][1], call))
        calls.append(call)
    calls.append(index_logits(blocks[4], iq, weights))
    losses, key_grad = loss_and_grad(me, doc_start, queries[0], sum(blocks, []), calls, iq, weights)

    key_grad = lax.all_to_all(key_grad, "ctx", 0, 0, tiled=True).reshape(16, ROWS, ID)
    own_grad = jnp.sum(key_grad.astype(jnp.float32), axis=0).astype(jnp.bfloat16)
    other_grad = lax.ppermute(own_grad, "dp", CORES)
    proj_part = lax.dot_general(
        jnp.concatenate([kept, taken], 0), jnp.concatenate([own_grad, other_grad], 0),
        (((0,), (0,)), ((), ())), preferred_element_type=jnp.float32,
    ).astype(jnp.bfloat16)
    proj_part = lax.all_to_all(proj_part, "dp", 0, 0, tiled=True, axis_index_groups=GROUPS)
    proj_part = jnp.sum(proj_part.reshape(8, -1, ID).astype(jnp.float32), axis=0)
    proj_part = lax.all_to_all(proj_part, "ctx", 0, 0, tiled=True)
    proj_grad = jnp.sum(proj_part.reshape(16, -1, ID), axis=0)
    return (losses, proj_grad)


def solution(mesh):
    return jax.shard_map(
        shards,
        mesh=mesh,
        in_specs=(
            P("dp", "ctx", None),
            P("dp", None, "ctx"),
            P("dp", "ctx", None),
            P(),
            P("dp", "ctx", None),
            P("dp", "ctx", None),
            P("dp", None),
        ),
        out_specs=(P("dp", "ctx"), P(("dp", "ctx"), None)),
        check_vma=False,
    )
```
